256 devices in a mesh: pre: 8 (over y, core), wide: 32 (over x, z).
Axes of the slice: x: 4, y: 4, z: 8, core: 2. Of those that a mesh axis runs over, the one named last changes fastest.
Arguments:
- prompt_hidden: bfloat16 [16384, 8192], P('wide', 'pre'), may hold values from -6 to 6
- attn_gain: float32 [8192], replicated, may hold values from 0.25 to 1.75
- kv_weight: bfloat16 [8192, 2048], P(None, 'pre'), may hold values from -0.0625 to 0.0625
- prompt_lengths: int32 [512], P('wide'), may hold values from 1 to 32, as said below
- owner_slot: int32 [512], P('wide'), may hold values from 0 to 511, as said below
- new_queries: bfloat16 [1, 512, 8192], P(None, 'wide', 'pre'), may hold values from -60 to 60
- new_keys_values: bfloat16 [1, 512, 2048], P(None, 'wide', 'pre'), may hold values from -8 to 8
- out_weight: bfloat16 [8192, 8192], P('pre', 'wide'), may hold values from -0.0625 to 0.0625
- residual: bfloat16 [1, 512, 8192], P(None, None, 'wide'), may hold values from -6 to 6
- final_gain: float32 [8192], P('wide'), may hold values from 0.25 to 1.75
- vocab_weight: bfloat16 [8192, 65536], P('wide', 'pre'), may hold values from -3 to 3
- sampled_ids: int32 [1, 512], replicated, may hold values from 0 to 65535
Outputs:
- logprobs: float32 [1, 512], P(None, 'wide')
The draws below stay inside these ranges and needn't reach their ends.
Inputs may be any that keep to these rules, and one draw needn't show every extreme that they name: `prompt_lengths`: some request has a prompt of exactly 32 positions. `owner_slot`: A permutation of the 512 decode rows; decode row o is owned by wide index o // 16. Each wide index owns 16 rows, and no two requests prefilled on one wide index go to the same owner.
All inputs are finite; a program needn't handle non-finite values.
Results may differ from the reference program's by a relative error of at most 0.003.
Values may be sent and summed in bfloat16 or wider, within the bound.
No kernel may reach another device: no remote copies, remote signals or barrier semaphores. Data moves between devices by JAX's collectives and lax.ppermute only.
A program may use at most 128 MiB of HBM per device.

```python
import math
import jax
import jax.numpy as jnp
from jax import lax

D = 8192
HEADS = 64
KV_HEADS = 8
HEAD_DIM = 128
VOCAB = 65536
CACHE_LEN = 32
STEPS = 1
REQ_DEV = 16
REQUESTS = 512
TOKENS = 16384
N_WIDE = 32


def decode_pair(key):
    query_key, pair_key = jax.random.split(key)
    pairs = jax.random.normal(pair_key, (STEPS, REQUESTS, KV_HEADS, 2, HEAD_DIM), jnp.float32)
    pairs = jnp.clip(pairs, -6.0, 6.0)
    queries = jax.random.normal(query_key, (STEPS, REQUESTS, KV_HEADS, HEADS // KV_HEADS, HEAD_DIM), jnp.float32)
    queries = jnp.clip(queries, -6.0, 6.0)
    return (queries, pairs)


def draw_prompt_lengths(key, part):
    key = jax.random.fold_in(key, 11)
    length_key, spot_key = jax.random.split(key)
    lengths = jax.random.randint(length_key, (REQUESTS,), 1, CACHE_LEN + 1)
    spot = jax.random.randint(spot_key, (), 0, REQUESTS)
    return lengths.at[spot].set(CACHE_LEN).astype(jnp.int32)


def draw_owner_slot(key, part):
    key = jax.random.fold_in(key, 12)
    base_key, offset_key, slot_key = jax.random.split(key, 3)
    base_order = jax.random.permutation(base_key, N_WIDE)
    offsets = jax.random.permutation(offset_key, N_WIDE)[:REQ_DEV]
    source = jnp.arange(REQUESTS, dtype=jnp.int32) // REQ_DEV
    within = jnp.arange(REQUESTS, dtype=jnp.int32) % REQ_DEV
    owner = (base_order[source] + offsets[within]) % N_WIDE
    slot_orders = jax.vmap(lambda one_key: jax.random.permutation(one_key, REQ_DEV))(jax.random.split(slot_key, N_WIDE))
    slot = slot_orders[owner, within]
    return (owner * REQ_DEV + slot).astype(jnp.int32)


def draw_new_queries(key, part):
    queries, pairs = decode_pair(key)
    queries = jnp.clip(queries, -60.0, 60.0)
    return queries.reshape(STEPS, REQUESTS, HEADS * HEAD_DIM).astype(jnp.bfloat16)


def draw_new_keys_values(key, part):
    queries, pairs = decode_pair(key)
    return pairs.reshape(STEPS, REQUESTS, KV_HEADS * 2 * HEAD_DIM).astype(jnp.bfloat16)


def draw_vocab_weight(key, part):
    key = jax.random.fold_in(key, 15)
    base_key = jax.random.fold_in(key, 0)
    base = jnp.clip(jax.random.normal(base_key, (D, VOCAB), jnp.float32), -6.0, 6.0)
    weights = base * 3.0 / math.sqrt(D)
    return jnp.clip(weights, -3.0, 3.0).astype(jnp.bfloat16)


def plant(entries, rng, low, top_value):
    longest = entries.shape.index(max(entries.shape))
    spots = []
    for shift in (0, 1):
        where = [jax.random.randint(jax.random.fold_in(rng, axis), (), 0, length) for axis, length in enumerate(entries.shape)]
        where[longest] = (where[longest] + shift) % entries.shape[longest]
        spots.append(tuple(where))
    return entries.at[spots[0]].set(low).at[spots[1]].set(top_value)


def block_scale(stream_key, dims, cuts, low, high):
    def one(dim, parts):
        draws = jax.random.uniform(jax.random.fold_in(jax.random.fold_in(stream_key, 6), dim), (parts,), jnp.float32, low / len(cuts), high / len(cuts))
        return jnp.repeat(jnp.exp(draws), dims[dim] // parts).reshape((-1,) + (1,) * (len(dims) - dim - 1))

    level = one(*cuts[0])
    for cut in cuts[1:]:
        level = level * one(*cut)
    return level


def gaussian(key, dims, scale, limit, cuts=(), held_as=jnp.bfloat16):
    values = jax.random.normal(key, dims, jnp.float32) * scale
    if len(cuts) > 0:
        values = block_scale(key, dims, cuts, -0.22, 0.18) * values
    return jnp.clip(values, min=-limit, max=limit).astype(held_as)


def setup_inputs(seed: int = 0) -> dict:
    arg_keys = jax.random.split(jax.random.key(seed), 13)
    return {
        "prompt_hidden": gaussian(arg_keys[0], (TOKENS, D), 1.0, 6.0, ((0, 32), (1, 8))),
        "attn_gain": jnp.clip(1.0 + 0.15 * jax.random.normal(arg_keys[1], (D,), jnp.float32), 0.25, 1.75),
        "kv_weight": gaussian(arg_keys[2], (D, KV_HEADS * 2 * HEAD_DIM), D ** -0.5, 0.0625, ((1, 8),)),
        "prompt_lengths": draw_prompt_lengths(jax.random.fold_in(arg_keys[12], 71), 0),
        "owner_slot": draw_owner_slot(jax.random.fold_in(arg_keys[12], 71), 0),
        "new_queries": draw_new_queries(jax.random.fold_in(arg_keys[12], 71), 0),
        "new_keys_values": draw_new_keys_values(jax.random.fold_in(arg_keys[12], 71), 0),
        "out_weight": gaussian(arg_keys[7], (HEADS * HEAD_DIM, D), (HEADS * HEAD_DIM) ** -0.5, 0.0625, ((0, 8), (1, 32))),
        "residual": gaussian(arg_keys[8], (STEPS, REQUESTS, D), 1.0, 6.0, ((2, 32),)),
        "final_gain": jnp.clip(1.0 + 0.15 * jax.random.normal(arg_keys[9], (D,), jnp.float32), 0.25, 1.75),
        "vocab_weight": draw_vocab_weight(jax.random.fold_in(arg_keys[12], 71), 0),
        "sampled_ids": plant(jax.random.randint(arg_keys[11], (STEPS, REQUESTS), 0, VOCAB), jax.random.fold_in(arg_keys[11], 1), 0, VOCAB - 1).astype(jnp.int32),
    }


epsilon = 1e-05
rope_base = 500000.0

def rotate(values_in, positions):
    half_dim = values_in.shape[-1] // 2
    frequency = rope_base ** (-jnp.arange(half_dim, dtype=jnp.float32) / half_dim)
    angles = positions[..., None] * frequency
    cosine = jnp.cos(angles)
    sine_part = jnp.sin(angles)
    first_half = values_in[..., :half_dim]
    second_half = values_in[..., half_dim:]
    return jnp.concatenate([first_half * cosine - second_half * sine_part, second_half * cosine + first_half * sine_part], axis=-1)

def attend(queries, new_pairs, cache_keys, cache_values, lengths):
    num_steps = queries.shape[0]
    cache_len = cache_keys.shape[1]
    positions = (lengths[None, :] + jnp.arange(num_steps, dtype=jnp.int32)[:, None]).astype(jnp.float32)
    rotated = rotate(queries.astype(jnp.float32), positions[:, :, None, None])
    new_keys = rotate(new_pairs[:, :, :, 0].astype(jnp.float32), positions[:, :, None])
    new_values = new_pairs[:, :, :, 1].astype(jnp.float32)
    factor = queries.shape[-1] ** (-0.5)
    cache_scores = jnp.einsum('srkgd,rckd->srkgc', rotated, cache_keys.astype(jnp.float32)) * factor
    live = jnp.arange(cache_len, dtype=jnp.int32)[None, :] < lengths[:, None]
    cache_scores = jnp.where(live[None, :, None, None, :], cache_scores, -1e+30)
    own_scores = jnp.einsum('srkgd,urkd->srkgu', rotated, new_keys) * factor
    causal = jnp.arange(num_steps)[None, :] <= jnp.arange(num_steps)[:, None]
    own_scores = jnp.where(causal[:, None, None, None, :], own_scores, -1e+30)
    scores = jnp.concatenate([cache_scores, own_scores], axis=-1)
    row_max = lax.optimization_barrier(jnp.max(scores, axis=-1, keepdims=True))
    weights = jnp.exp(scores - row_max)
    weights = (weights / lax.optimization_barrier(jnp.sum(weights, axis=-1, keepdims=True))).astype(jnp.bfloat16)
    mixed = jnp.einsum('srkgc,rckd->srkgd', weights[..., :cache_len].astype(jnp.float32), cache_values.astype(jnp.float32))
    mixed = mixed + jnp.einsum('srkgu,urkd->srkgd', weights[..., cache_len:].astype(jnp.float32), new_values)
    return mixed.astype(jnp.bfloat16)

def reference(prompt_hidden, attn_gain, kv_weight, prompt_lengths, owner_slot, new_queries, new_keys_values, out_weight, residual, final_gain, vocab_weight, sampled_ids):
    hidden_wide = prompt_hidden.astype(jnp.float32)
    norm_factor = lax.rsqrt(lax.optimization_barrier(jnp.mean(hidden_wide * hidden_wide, axis=-1, keepdims=True)) + epsilon)
    normed = (hidden_wide * norm_factor * attn_gain).astype(jnp.bfloat16)
    projected = jnp.dot(normed, kv_weight, preferred_element_type=jnp.float32)
    projected = projected.reshape(REQUESTS, CACHE_LEN, KV_HEADS, 2, HEAD_DIM)
    cache_positions = jnp.arange(CACHE_LEN, dtype=jnp.int32).astype(jnp.float32)
    cache_keys = rotate(projected[:, :, :, 0], cache_positions[None, :, None]).astype(jnp.bfloat16)
    cache_values = projected[:, :, :, 1].astype(jnp.bfloat16)
    source_of = jnp.zeros((REQUESTS,), jnp.int32).at[owner_slot].set(jnp.arange(REQUESTS, dtype=jnp.int32))
    owned_keys = cache_keys[source_of]
    owned_values = cache_values[source_of]
    owned_lengths = prompt_lengths[source_of]
    queries = new_queries.reshape(STEPS, REQUESTS, KV_HEADS, HEADS // KV_HEADS, HEAD_DIM)
    new_pairs = new_keys_values.reshape(STEPS, REQUESTS, KV_HEADS, 2, HEAD_DIM)
    attended = attend(queries, new_pairs, owned_keys, owned_values, owned_lengths)
    attended = attended.reshape(STEPS * REQUESTS, HEADS * HEAD_DIM)
    updated = residual.astype(jnp.float32) + jnp.dot(attended, out_weight, preferred_element_type=jnp.float32).reshape(STEPS, REQUESTS, D)
    squares = lax.optimization_barrier(jnp.sum(updated * updated, axis=-1))
    gained = (updated * final_gain).astype(jnp.bfloat16)
    logits = jnp.dot(gained.reshape(STEPS * REQUESTS, D), vocab_weight, preferred_element_type=jnp.float32)
    logits = logits.reshape(STEPS, REQUESTS, VOCAB) * lax.rsqrt(squares / D + epsilon)[..., None]
    row_max = lax.optimization_barrier(jnp.max(logits, axis=-1))
    log_total = row_max + jnp.log(lax.optimization_barrier(jnp.sum(jnp.exp(logits - row_max[..., None]), axis=-1)))
    picked = jnp.take_along_axis(logits, sampled_ids[..., None], axis=-1)[..., 0]
    return picked - log_total
```

```python
import functools

import jax
import jax.numpy as jnp
import numpy as np
from jax import lax
from jax.experimental import pallas as pl
from jax.experimental.pallas import tpu as pltpu
from jax.sharding import Mesh, PartitionSpec as P

HEAD_DIM = 128
LANES = 128
CORES = 2
X = 4
LOW = 2

epsilon = 1e-05
rope_base = 500000.0

f32 = jnp.float32
bf16 = jnp.bfloat16


def rope_turns(positions, xp=jnp):
    half_dim = HEAD_DIM // 2
    frequency = rope_base ** (-np.arange(half_dim) / half_dim)
    angles = positions.astype(f32)[:, None] * frequency.astype(np.float32)
    cosine = xp.cos(angles)
    sine = xp.sin(angles)
    return xp.stack(
        [
            xp.concatenate([cosine, cosine], axis=1),
            xp.concatenate([-sine, sine], axis=1),
        ]
    )


def shift(value, axis, step):
    count = lax.axis_size(axis)
    return lax.ppermute(value, axis, [(i, (i + step) % count) for i in range(count)])


def swap(value):
    return shift(value, "c", 1)


def rows_at(value, start, count):
    return lax.dynamic_slice_in_dim(value, start, count, 0)


def in_three(value):
    high = lax.reduce_precision(value, 8, 7)
    rest = value - high
    middle = lax.reduce_precision(rest, 8, 7)
    return high.astype(bf16), middle.astype(bf16), (rest - middle).astype(bf16)


def dot(a, b):
    return jnp.dot(a, b, preferred_element_type=f32)


def dot_t(a, b):
    return lax.dot_general(a, b, (((1,), (1,)), ((), ())), preferred_element_type=f32)


def attend_kernel(
    width,
    cache_len,
    hidden_ref,
    weight_ref,
    gain_ref,
    key_turns_ref,
    picked_ref,
    turns_ref,
    lengths_ref,
    out_ref,
    sums_ref,
    squares_ref,
):
    step = pl.program_id(0)
    wide = hidden_ref[0].astype(f32)
    squares = jnp.sum(wide * wide, axis=1, keepdims=True)
    sums = dot((wide * gain_ref[0]).astype(bf16), weight_ref[...])

    @pl.when(step == 0)
    def _():
        sums_ref[...] = sums
        squares_ref[...] = squares

    @pl.when(step > 0)
    def _():
        sums_ref[...] += sums
        squares_ref[...] += squares

    @pl.when(step == pl.num_programs(0) - 1)
    def _():
        norm_factor = lax.rsqrt(squares_ref[...] * (1.0 / width) + epsilon)
        projected = sums_ref[...] * norm_factor
        requests = lengths_ref.shape[0]
        tokens = projected.shape[0]
        picked = picked_ref[...].astype(f32)
        groups = picked.shape[1] // HEAD_DIM - 2
        factor = HEAD_DIM ** (-0.5)

        def turned(rows, turns):
            return rows * turns[0] + pltpu.roll(rows, HEAD_DIM // 2, 1) * turns[1]

        columns = [picked[:, g * HEAD_DIM : (g + 1) * HEAD_DIM] for g in range(groups + 2)]
        queries = [turned(rows, turns_ref) for rows in columns[:groups]]
        new_key = turned(columns[groups], turns_ref)
        own = [jnp.sum(rows * new_key, axis=1, keepdims=True) * factor for rows in queries]
        own = jnp.concatenate(own, axis=0)
        queries = jnp.concatenate(queries, axis=0)
        new_values = jnp.concatenate([columns[groups + 1]] * groups, axis=0)
        token = lax.broadcasted_iota(jnp.int32, (requests, tokens), 1)
        request = lax.broadcasted_iota(jnp.int32, (requests, tokens), 0)
        start = request * cache_len
        live = (token >= start) & (token < start + lengths_ref[...])
        bias = jnp.where(live, 0.0, -1e30)
        bias = jnp.concatenate([bias] * groups, axis=0)
        keys = turned(projected[:, :HEAD_DIM], key_turns_ref).astype(bf16)
        values = projected[:, HEAD_DIM:].astype(bf16)
        upper = queries.astype(bf16)
        lower = (queries - upper.astype(f32)).astype(bf16)
        scores = (dot_t(upper, keys) + dot_t(lower, keys)) * factor + bias
        row_max = jnp.maximum(jnp.max(scores, axis=1, keepdims=True), own)
        weights = jnp.exp(scores - row_max)
        own_weight = jnp.exp(own - row_max)
        total = jnp.sum(weights, axis=1, keepdims=True) + own_weight
        weights = (weights / total).astype(bf16)
        own_weight = (own_weight / total).astype(bf16).astype(f32)
        mixed = dot(weights, values) + own_weight * new_values
        pieces = [mixed[g * requests : (g + 1) * requests] for g in range(groups)]
        mixed = jnp.concatenate(pieces, axis=1).astype(bf16)
        out_ref[...] = jnp.broadcast_to(mixed[None], out_ref.shape)


def three_columns(value):
    column = lax.broadcasted_iota(jnp.int32, (value.shape[0], LANES), 1)
    terms = jnp.zeros((value.shape[0], LANES), f32)
    for place, term in enumerate(in_three(value)):
        terms = jnp.where(column == place, term.astype(f32), terms)
    return terms.astype(bf16)


def logits_kernel(decode_shape, place_ref, gains_ref, order_ref, *refs):
    outs = decode_shape[0]
    held = (len(refs) - outs) // 2
    from_refs, out_refs = refs[:held], refs[held : held + outs]
    held_refs, sems = refs[held + outs : -1], refs[-1]
    copies = [
        pltpu.make_async_copy(from_ref, held_ref, sems.at[index])
        for index, (from_ref, held_ref) in enumerate(zip(from_refs, held_refs))
    ]
    for copy in copies:
        copy.start()
    weight_refs = held_refs[2:]
    depth, out_cols = weight_refs[0].shape
    parts = held_refs[0].shape[0]
    lows = len(weight_refs) // parts
    inverse = [1.0 / gains_ref[index] for index in range(parts)]
    squares = []
    for copy, rows_ref in zip(copies[:2], held_refs[:2]):
        copy.wait()
        total = jnp.zeros(rows_ref.shape[1:], f32)
        for index in range(parts):
            updated = rows_ref[index].astype(f32) * inverse[index]
            total = total + updated * updated
        squares.append(three_columns(jnp.sum(total, axis=1, keepdims=True)))
    totals = [None, None]
    for index, weight_ref in enumerate(weight_refs):
        place = lax.rem(place_ref[2] - index // lows + parts, parts)
        low = lax.rem(place_ref[1] + index % lows, lows)
        start = pl.multiple_of(low * depth, depth)
        copies[2 + index].wait()
        for half, rows_ref in enumerate(held_refs[:2]):
            term = dot(rows_ref[place, :, pl.ds(start, depth)], weight_ref[...])
            totals[half] = term if index == 0 else totals[half] + term
    high_count, x_count, low_count, requests = decode_shape
    rows = order_ref.shape[1]
    row = lax.broadcasted_iota(jnp.int32, (rows, rows), 0)
    within = row % (low_count * requests)
    x_place = row // (low_count * requests) % x_count
    high_place = (row // (low_count * requests * x_count) + place_ref[3]) % high_count
    decode_row = (x_place * high_count + high_place) * (low_count * requests) + within
    permutation = (decode_row == order_ref[...]).astype(f32).astype(bf16)
    logits = jnp.concatenate([total.astype(bf16) for total in totals], axis=0)
    logits = dot(permutation, logits).astype(bf16)
    squares = dot(permutation, jnp.concatenate(squares, axis=0)).astype(bf16)
    block = rows // outs
    for index, out_ref in enumerate(out_refs):
        out_ref[:, :out_cols] = logits[index * block : (index + 1) * block]
        out_ref[:, out_cols:] = squares[index * block : (index + 1) * block]


def project_kernel(place_ref, rows_ref, mine_ref, near_ref, kept_ref, given_ref):
    core = place_ref[0]
    low = place_ref[1]
    groups, requests, depth = rows_ref.shape
    rows = rows_ref[...].reshape(groups * requests, depth)
    mine = dot(rows, mine_ref[...])
    near = dot(rows, near_ref[...])
    terms = jnp.concatenate(
        [jnp.where(low == 0, mine, near), jnp.where(low == 0, near, mine)], axis=1
    )
    terms = terms.reshape(groups, CORES, requests // CORES, terms.shape[1])
    first, second = terms[:, 0], terms[:, 1]
    kept_ref[...] = jnp.where(core == 0, first, second)
    given_ref[...] = jnp.where(core == 0, second, first)


def local(
    prompt_hidden,
    attn_gain,
    kv_weight,
    prompt_lengths,
    owner_slot,
    new_queries,
    new_keys_values,
    out_weight,
    residual,
    final_gain,
    vocab_weight,
    sampled_ids,
):
    core = lax.axis_index("c")
    y = lax.axis_index("y")
    x = lax.axis_index("x")
    high = lax.axis_index("h")
    low = lax.axis_index("l")
    y_count = lax.axis_size("y")
    x_count = lax.axis_size("x")
    high_count = lax.axis_size("h")
    low_count = lax.axis_size("l")
    z_count = high_count * low_count
    wide = x_count * z_count
    z = high * low_count + low
    me = x * z_count + z
    wide_axes = ("x", "h", "l")

    width = attn_gain.shape[0]
    requests = prompt_lengths.shape[0]
    half = requests // CORES
    total_rows = requests * wide
    cache_len = prompt_hidden.shape[0] // requests
    tokens = prompt_hidden.shape[0]
    depth = prompt_hidden.shape[1]

    hidden = lax.all_gather(prompt_hidden, ("y", "c"), axis=0)

    columns = out_weight.shape[1]
    vocab_local = vocab_weight.shape[1]
    group = low_count * x_count
    vocab_cols = vocab_local // group

    def sent_block(vocab_weight, d, e):
        place = lax.rem(x + d, x_count) * low_count + lax.rem(low + e, low_count)
        return lax.dynamic_slice_in_dim(vocab_weight, place * vocab_cols, vocab_cols, 1)

    def moved(block, d, e):
        pairs = [
            (i * low_count + j, (i + d) % x_count * low_count + (j + e) % low_count)
            for i in range(x_count)
            for j in range(low_count)
        ]
        return lax.ppermute(block, ("x", "l"), pairs)

    first_places = [(1, 0), (3, 0)]
    vocab_blocks = {place: sent_block(vocab_weight, *place) for place in first_places}
    vocab_later, prompt_lengths = lax.optimization_barrier((vocab_weight, prompt_lengths))
    for d in range(x_count):
        for e in range(low_count):
            if (d, e) not in vocab_blocks:
                vocab_blocks[d, e] = sent_block(vocab_later, d, e)

    told = jnp.concatenate([owner_slot.astype(f32), final_gain])
    width_told = -(-told.shape[0] // LANES) * LANES
    told = jnp.pad(told, (0, width_told - told.shape[0]))
    told = lax.all_to_all(
        jnp.broadcast_to(told[None, None, :], (wide, 1, width_told)),
        wide_axes,
        0,
        0,
        tiled=True,
    )

    def phase(places, *others):
        done = {place: moved(vocab_blocks[place], *place) for place in places}
        done, others, waiting = lax.optimization_barrier(
            (done, others, {k: v for k, v in vocab_blocks.items() if k not in done})
        )
        vocab_blocks.update(done)
        vocab_blocks.update(waiting)
        return others

    told, out_near = phase(first_places, told, shift(out_weight, "l", 1))
    owners = told[:, :, :requests].astype(jnp.int32)

    decode_rows = jnp.concatenate([new_queries[0], new_keys_values[0]], axis=1)
    own_rows = me * requests + jnp.arange(requests, dtype=jnp.int32)
    wanted = jnp.any(owners == own_rows[None, :, None], axis=2).astype(bf16)
    outgoing = dot(wanted, decode_rows).astype(bf16)
    incoming = lax.all_to_all(outgoing[:, None, :], wide_axes, 0, 0, tiled=True)
    told, incoming = phase([(1, 1), (3, 1)], told, incoming)
    owners = told[:, :, :requests].astype(jnp.int32)
    gains = told[:, 0, requests : requests + columns]
    gains = gains.reshape(x_count, high_count, low_count * columns)
    gains = lax.dynamic_index_in_dim(gains, high, 1)
    incoming = incoming[:, 0]
    pick = (owner_slot // requests)[:, None] == jnp.arange(wide, dtype=jnp.int32)[None, :]
    picked = dot(pick.astype(bf16), incoming).astype(bf16)
    head_width = new_queries.shape[2]

    row_block = requests // CORES * high_count
    by_place = owners.reshape(x_count, high_count, low_count, CORES, half)
    here = lax.dynamic_index_in_dim(by_place, y, 0, keepdims=False)
    here = lax.dynamic_index_in_dim(here, core, 2, keepdims=False)
    decode_index = jnp.arange(total_rows, dtype=jnp.int32)

    def residual_rows(place):
        rows = lax.dynamic_index_in_dim(here, place, 1, keepdims=False).reshape(-1)
        pick = (rows[:, None] == decode_index[None, :]).astype(bf16)
        return dot(pick, residual[0]).astype(bf16)

    def of_pair(mine, near):
        return jnp.where(
            low == 0,
            jnp.concatenate([mine, near], axis=1),
            jnp.concatenate([near, mine], axis=1),
        )

    residual_here = of_pair(
        residual_rows(low), shift(residual_rows(1 - low), "l", 1)
    ).astype(f32)
    gain_here = lax.dynamic_index_in_dim(gains, x, 0, keepdims=False)

    blocks = hidden.shape[0]
    places = x_count * high_count
    kv_columns = kv_weight.shape[1]

    def whole(*shape):
        return pl.BlockSpec(shape, lambda step: (0,) * len(shape))

    attended = pl.pallas_call(
        functools.partial(attend_kernel, width, cache_len),
        grid=(blocks,),
        out_shape=jax.ShapeDtypeStruct((places, requests, head_width), bf16),
        in_specs=[
            pl.BlockSpec((1, tokens, depth), lambda step: (step, 0, 0)),
            pl.BlockSpec((depth, kv_columns), lambda step: (step, 0)),
            pl.BlockSpec((1, 1, depth), lambda step: (step, 0, 0)),
            whole(2, tokens, HEAD_DIM),
            whole(requests, head_width + kv_columns),
            whole(2, requests, HEAD_DIM),
            whole(requests, 1),
        ],
        out_specs=whole(places, requests, head_width),
        scratch_shapes=[pltpu.VMEM((tokens, kv_columns), f32), pltpu.VMEM((tokens, 1), f32)],
        compiler_params=pltpu.CompilerParams(vmem_limit_bytes=60 * 1024 * 1024),
    )(
        hidden,
        kv_weight,
        attn_gain.reshape(blocks, 1, depth),
        rope_turns(np.arange(tokens) % cache_len, np),
        picked,
        rope_turns(prompt_lengths),
        prompt_lengths[:, None],
    )

    (attended,) = phase([(2, 0), (2, 1), (0, 1)], attended)
    attended = lax.all_to_all(attended, ("x", "h"), 0, 0, tiled=True)
    place = jnp.stack([core, low, x, high]).astype(jnp.int32)
    smem = pl.BlockSpec(memory_space=pltpu.SMEM)
    vmem = pl.BlockSpec(memory_space=pltpu.VMEM)
    part = jax.ShapeDtypeStruct((places, half, low_count * columns), f32)
    kept, given = pl.pallas_call(
        project_kernel,
        out_shape=(part, part),
        in_specs=[smem, vmem, vmem, vmem],
        out_specs=(vmem, vmem),
        compiler_params=pltpu.CompilerParams(vmem_limit_bytes=24 * 1024 * 1024),
    )(place, attended, out_weight, out_near)
    terms = (kept + swap(given)).reshape(x_count * row_block, -1)
    updated = residual_here + rows_at(terms, y * row_block, row_block)
    for step in range(1, y_count):
        part = rows_at(terms, lax.rem(y + step, y_count) * row_block, row_block)
        updated = updated + shift(part, "y", step)
    gained = (updated * gain_here).astype(bf16)

    count = x_count * low_count * y_count
    gathered = lax.all_to_all(
        jnp.broadcast_to(gained[None], (count,) + gained.shape), ("x", "l", "y"), 0, 0, tiled=True
    )
    gathered = gathered.reshape(x_count, count // x_count * row_block, -1)

    request_order = jnp.transpose(by_place, (3, 2, 0, 1, 4))
    request_order = jnp.where(core == 0, request_order, request_order[::-1]).reshape(-1)
    weights = [vocab_blocks[d, e] for d in range(x_count) for e in range(low_count)]
    operands = [gathered, swap(gathered)] + weights
    part = jax.ShapeDtypeStruct((total_rows // high_count, vocab_cols + LANES), bf16)
    partial = pl.pallas_call(
        functools.partial(logits_kernel, (high_count, x_count, low_count, requests)),
        out_shape=(part,) * high_count,
        in_specs=[smem, vmem, vmem] + [pl.BlockSpec(memory_space=pl.ANY)] * len(operands),
        out_specs=(vmem,) * high_count,
        scratch_shapes=[pltpu.VMEM(value.shape, bf16) for value in operands]
        + [pltpu.SemaphoreType.DMA((len(operands),))],
        compiler_params=pltpu.CompilerParams(vmem_limit_bytes=60 * 1024 * 1024),
    )(place, gains, request_order[None, :], *operands)
    parts = [partial[0]] + [shift(partial[d], "h", d) for d in (2, 1, 3)]
    summed = sum(value.astype(f32) for value in parts)
    own_squares = jnp.sum(summed[:, vocab_cols : vocab_cols + 3], axis=1, keepdims=True)
    logits = summed[:, :vocab_cols] * lax.rsqrt(own_squares / width + epsilon)

    id_rows = sampled_ids.reshape(x_count, high_count, low_count, requests)
    id_rows = lax.dynamic_index_in_dim(id_rows, high, 1, keepdims=False).reshape(-1)
    first = (y * CORES + core) * vocab_local + (x * low_count + low) * vocab_cols
    column_ids = first + jnp.arange(vocab_cols, dtype=jnp.int32)
    highest = jnp.max(logits, axis=-1)
    summed_exp = jnp.sum(jnp.exp(logits - highest[:, None]), axis=-1)
    target = jnp.sum(jnp.where(column_ids[None, :] == id_rows[:, None], logits, 0.0), axis=-1)
    stats = jnp.stack([highest, summed_exp, target]).reshape(3, group, requests)
    stats = jnp.transpose(stats, (1, 0, 2)).reshape(group, 3 * requests)
    stats = jnp.pad(stats, ((0, 0), (0, LANES - 3 * requests)))
    ends = y_count * CORES
    stats = jnp.broadcast_to(stats[None], (ends, group, LANES)).reshape(ends * group, 1, LANES)
    stats = lax.all_to_all(stats, ("y", "c", "x", "l"), 0, 0, tiled=True)[:, 0]
    all_highest = stats[:, :requests]
    top = jnp.max(all_highest, axis=0)
    sum_all = jnp.sum(
        stats[:, requests : 2 * requests] * jnp.exp(all_highest - top[None, :]), axis=0
    )
    target_all = jnp.sum(stats[:, 2 * requests : 3 * requests], axis=0)
    return (target_all - top - jnp.log(sum_all))[None, :]


def solution(mesh):
    pre, wide = mesh.devices.shape
    shape = (pre // CORES, CORES, X, wide // X // LOW, LOW)
    fine = Mesh(mesh.devices.reshape(shape), ("y", "c", "x", "h", "l"))
    pre_axes = ("y", "c")
    wide_axes = ("x", "h", "l")
    return jax.shard_map(
        local,
        mesh=fine,
        in_specs=(
            P(wide_axes, pre_axes),
            P(),
            P(None, pre_axes),
            P(wide_axes),
            P(wide_axes),
            P(None, wide_axes, pre_axes),
            P(None, wide_axes, pre_axes),
            P(pre_axes, wide_axes),
            P(None, None, wide_axes),
            P(wide_axes),
            P(wide_axes, pre_axes),
            P(),
        ),
        out_specs=P(None, wide_axes),
        check_vma=False,
    )
```

```python
import functools

import jax
import jax.numpy as jnp
import numpy as np
from jax import lax
from jax.experimental import pallas as pl
from jax.experimental.pallas import tpu as pltpu
from jax.sharding import Mesh, PartitionSpec as P

HEAD_DIM = 128
LANES = 128
CORES = 2
X = 4
LOW = 2

epsilon = 1e-05
rope_base = 500000.0

f32 = jnp.float32
bf16 = jnp.bfloat16


def rope_turns(positions, xp=jnp):
    half_dim = HEAD_DIM // 2
    frequency = rope_base ** (-np.arange(half_dim) / half_dim)
    angles = positions.astype(f32)[:, None] * frequency.astype(np.float32)
    cosine = xp.cos(angles)
    sine = xp.sin(angles)
    return xp.stack(
        [
            xp.concatenate([cosine, cosine], axis=1),
            xp.concatenate([-sine, sine], axis=1),
        ]
    )


def shift(value, axis, step):
    count = lax.axis_size(axis)
    return lax.ppermute(value, axis, [(i, (i + step) % count) for i in range(count)])


def swap(value):
    return shift(value, "c", 1)


def rows_at(value, start, count):
    return lax.dynamic_slice_in_dim(value, start, count, 0)


def in_three(value):
    high = lax.reduce_precision(value, 8, 7)
    rest = value - high
    middle = lax.reduce_precision(rest, 8, 7)
    return high.astype(bf16), middle.astype(bf16), (rest - middle).astype(bf16)


def dot(a, b):
    return jnp.dot(a, b, preferred_element_type=f32)


def dot_t(a, b):
    return lax.dot_general(a, b, (((1,), (1,)), ((), ())), preferred_element_type=f32)


def attend_kernel(
    width,
    cache_len,
    hidden_ref,
    weight_ref,
    gain_ref,
    key_turns_ref,
    picked_ref,
    turns_ref,
    lengths_ref,
    out_ref,
    sums_ref,
    squares_ref,
):
    step = pl.program_id(0)
    wide = hidden_ref[0].astype(f32)
    squares = jnp.sum(wide * wide, axis=1, keepdims=True)
    sums = dot((wide * gain_ref[0]).astype(bf16), weight_ref[...])

    @pl.when(step == 0)
    def _():
        sums_ref[...] = sums
        squares_ref[...] = squares

    @pl.when(step > 0)
    def _():
        sums_ref[...] += sums
        squares_ref[...] += squares

    @pl.when(step == pl.num_programs(0) - 1)
    def _():
        norm_factor = lax.rsqrt(squares_ref[...] * (1.0 / width) + epsilon)
        projected = sums_ref[...] * norm_factor
        requests = lengths_ref.shape[0]
        tokens = projected.shape[0]
        picked = picked_ref[...].astype(f32)
        groups = picked.shape[1] // HEAD_DIM - 2
        factor = HEAD_DIM ** (-0.5)

        def turned(rows, turns):
            return rows * turns[0] + pltpu.roll(rows, HEAD_DIM // 2, 1) * turns[1]

        columns = [picked[:, g * HEAD_DIM : (g + 1) * HEAD_DIM] for g in range(groups + 2)]
        queries = [turned(rows, turns_ref) for rows in columns[:groups]]
        new_key = turned(columns[groups], turns_ref)
        own = [jnp.sum(rows * new_key, axis=1, keepdims=True) * factor for rows in queries]
        own = jnp.concatenate(own, axis=0)
        queries = jnp.concatenate(queries, axis=0)
        new_values = jnp.concatenate([columns[groups + 1]] * groups, axis=0)
        token = lax.broadcasted_iota(jnp.int32, (requests, tokens), 1)
        request = lax.broadcasted_iota(jnp.int32, (requests, tokens), 0)
        start = request * cache_len
        live = (token >= start) & (token < start + lengths_ref[...])
        bias = jnp.where(live, 0.0, -1e30)
        bias = jnp.concatenate([bias] * groups, axis=0)
        keys = turned(projected[:, :HEAD_DIM], key_turns_ref).astype(bf16)
        values = projected[:, HEAD_DIM:].astype(bf16)
        upper = queries.astype(bf16)
        lower = (queries - upper.astype(f32)).astype(bf16)
        scores = (dot_t(upper, keys) + dot_t(lower, keys)) * factor + bias
        row_max = jnp.maximum(jnp.max(scores, axis=1, keepdims=True), own)
        weights = jnp.exp(scores - row_max)
        own_weight = jnp.exp(own - row_max)
        total = jnp.sum(weights, axis=1, keepdims=True) + own_weight
        weights = (weights / total).astype(bf16)
        own_weight = (own_weight / total).astype(bf16).astype(f32)
        mixed = dot(weights, values) + own_weight * new_values
        pieces = [mixed[g * requests : (g + 1) * requests] for g in range(groups)]
        mixed = jnp.concatenate(pieces, axis=1).astype(bf16)
        out_ref[...] = jnp.broadcast_to(mixed[None], out_ref.shape)


def three_columns(value):
    column = lax.broadcasted_iota(jnp.int32, (value.shape[0], LANES), 1)
    terms = jnp.zeros((value.shape[0], LANES), f32)
    for place, term in enumerate(in_three(value)):
        terms = jnp.where(column == place, term.astype(f32), terms)
    return terms.astype(bf16)


def logits_kernel(decode_shape, place_ref, gains_ref, order_ref, *refs):
    outs = decode_shape[0]
    held = (len(refs) - outs) // 2
    from_refs, out_refs = refs[:held], refs[held : held + outs]
    held_refs, sems = refs[held + outs : -1], refs[-1]
    copies = [
        pltpu.make_async_copy(from_ref, held_ref, sems.at[index])
        for index, (from_ref, held_ref) in enumerate(zip(from_refs, held_refs))
    ]
    for copy in copies:
        copy.start()
    weight_refs = held_refs[2:]
    depth, out_cols = weight_refs[0].shape
    parts = held_refs[0].shape[0]
    lows = len(weight_refs) // parts
    inverse = [1.0 / gains_ref[index] for index in range(parts)]
    squares = []
    for copy, rows_ref in zip(copies[:2], held_refs[:2]):
        copy.wait()
        total = jnp.zeros(rows_ref.shape[1:], f32)
        for index in range(parts):
            updated = rows_ref[index].astype(f32) * inverse[index]
            total = total + updated * updated
        squares.append(three_columns(jnp.sum(total, axis=1, keepdims=True)))
    totals = [None, None]
    for index, weight_ref in enumerate(weight_refs):
        place = lax.rem(place_ref[2] - index // lows + parts, parts)
        low = lax.rem(place_ref[1] + index % lows, lows)
        start = pl.multiple_of(low * depth, depth)
        copies[2 + index].wait()
        for half, rows_ref in enumerate(held_refs[:2]):
            term = dot(rows_ref[place, :, pl.ds(start, depth)], weight_ref[...])
            totals[half] = term if index == 0 else totals[half] + term
    high_count, x_count, low_count, requests = decode_shape
    rows = order_ref.shape[1]
    row = lax.broadcasted_iota(jnp.int32, (rows, rows), 0)
    within = row % (low_count * requests)
    x_place = row // (low_count * requests) % x_count
    high_place = (row // (low_count * requests * x_count) + place_ref[3]) % high_count
    decode_row = (x_place * high_count + high_place) * (low_count * requests) + within
    permutation = (decode_row == order_ref[...]).astype(f32).astype(bf16)
    logits = jnp.concatenate([total.astype(bf16) for total in totals], axis=0)
    logits = dot(permutation, logits).astype(bf16)
    squares = dot(permutation, jnp.concatenate(squares, axis=0)).astype(bf16)
    block = rows // outs
    for index, out_ref in enumerate(out_refs):
        out_ref[:, :out_cols] = logits[index * block : (index + 1) * block]
        out_ref[:, out_cols:] = squares[index * block : (index + 1) * block]


def project_kernel(place_ref, rows_ref, mine_ref, near_ref, kept_ref, given_ref):
    core = place_ref[0]
    low = place_ref[1]
    groups, requests, depth = rows_ref.shape
    rows = rows_ref[...].reshape(groups * requests, depth)
    mine = dot(rows, mine_ref[...])
    near = dot(rows, near_ref[...])
    terms = jnp.concatenate(
        [jnp.where(low == 0, mine, near), jnp.where(low == 0, near, mine)], axis=1
    )
    terms = terms.reshape(groups, CORES, requests // CORES, terms.shape[1])
    first, second = terms[:, 0], terms[:, 1]
    kept_ref[...] = jnp.where(core == 0, first, second)
    given_ref[...] = jnp.where(core == 0, second, first)


def local(
    prompt_hidden,
    attn_gain,
    kv_weight,
    prompt_lengths,
    owner_slot,
    new_queries,
    new_keys_values,
    out_weight,
    residual,
    final_gain,
    vocab_weight,
    sampled_ids,
):
    core = lax.axis_index("c")
    y = lax.axis_index("y")
    x = lax.axis_index("x")
    high = lax.axis_index("h")
    low = lax.axis_index("l")
    y_count = lax.axis_size("y")
    x_count = lax.axis_size("x")
    high_count = lax.axis_size("h")
    low_count = lax.axis_size("l")
    z_count = high_count * low_count
    wide = x_count * z_count
    z = high * low_count + low
    me = x * z_count + z
    wide_axes = ("x", "h", "l")

    width = attn_gain.shape[0]
    requests = prompt_lengths.shape[0]
    half = requests // CORES
    total_rows = requests * wide
    cache_len = prompt_hidden.shape[0] // requests
    tokens = prompt_hidden.shape[0]
    depth = prompt_hidden.shape[1]

    hidden = lax.all_gather(prompt_hidden, ("y", "c"), axis=0)

    columns = out_weight.shape[1]
    vocab_local = vocab_weight.shape[1]
    group = low_count * x_count
    vocab_cols = vocab_local // group

    def sent_block(vocab_weight, d, e):
        place = lax.rem(x + d, x_count) * low_count + lax.rem(low + e, low_count)
        return lax.dynamic_slice_in_dim(vocab_weight, place * vocab_cols, vocab_cols, 1)

    def moved(block, d, e):
        pairs = [
            (i * low_count + j, (i + d) % x_count * low_count + (j + e) % low_count)
            for i in range(x_count)
            for j in range(low_count)
        ]
        return lax.ppermute(block, ("x", "l"), pairs)

    first_places = [(1, 0), (3, 0)]
    vocab_blocks = {place: sent_block(vocab_weight, *place) for place in first_places}
    vocab_later, prompt_lengths = lax.optimization_barrier((vocab_weight, prompt_lengths))
    for d in range(x_count):
        for e in range(low_count):
            if (d, e) not in vocab_blocks:
                vocab_blocks[d, e] = sent_block(vocab_later, d, e)

    told = jnp.concatenate([owner_slot.astype(f32), final_gain])
    width_told = -(-told.shape[0] // LANES) * LANES
    told = jnp.pad(told, (0, width_told - told.shape[0]))
    told = lax.all_to_all(
        jnp.broadcast_to(told[None, None, :], (wide, 1, width_told)),
        wide_axes,
        0,
        0,
        tiled=True,
    )

    def phase(places, *others):
        done = {place: moved(vocab_blocks[place], *place) for place in places}
        done, others, waiting = lax.optimization_barrier(
            (done, others, {k: v for k, v in vocab_blocks.items() if k not in done})
        )
        vocab_blocks.update(done)
        vocab_blocks.update(waiting)
        return others

    told, out_near = phase(first_places, told, shift(out_weight, "l", 1))
    owners = told[:, :, :requests].astype(jnp.int32)

    decode_rows = jnp.concatenate([new_queries[0], new_keys_values[0]], axis=1)
    own_rows = me * requests + jnp.arange(requests, dtype=jnp.int32)
    wanted = jnp.any(owners == own_rows[None, :, None], axis=2).astype(bf16)
    outgoing = dot(wanted, decode_rows).astype(bf16)
    incoming = lax.all_to_all(outgoing[:, None, :], wide_axes, 0, 0, tiled=True)
    told, incoming = phase([(1, 1), (3, 1), (2, 0)], told, incoming)
    owners = told[:, :, :requests].astype(jnp.int32)
    gains = told[:, 0, requests : requests + columns]
    gains = gains.reshape(x_count, high_count, low_count * columns)
    gains = lax.dynamic_index_in_dim(gains, high, 1)
    incoming = incoming[:, 0]
    pick = (owner_slot // requests)[:, None] == jnp.arange(wide, dtype=jnp.int32)[None, :]
    picked = dot(pick.astype(bf16), incoming).astype(bf16)
    head_width = new_queries.shape[2]

    row_block = requests // CORES * high_count
    by_place = owners.reshape(x_count, high_count, low_count, CORES, half)
    here = lax.dynamic_index_in_dim(by_place, y, 0, keepdims=False)
    here = lax.dynamic_index_in_dim(here, core, 2, keepdims=False)
    decode_index = jnp.arange(total_rows, dtype=jnp.int32)

    def residual_rows(place):
        rows = lax.dynamic_index_in_dim(here, place, 1, keepdims=False).reshape(-1)
        pick = (rows[:, None] == decode_index[None, :]).astype(bf16)
        return dot(pick, residual[0]).astype(bf16)

    def of_pair(mine, near):
        return jnp.where(
            low == 0,
            jnp.concatenate([mine, near], axis=1),
            jnp.concatenate([near, mine], axis=1),
        )

    residual_here = of_pair(
        residual_rows(low), shift(residual_rows(1 - low), "l", 1)
    ).astype(f32)
    gain_here = lax.dynamic_index_in_dim(gains, x, 0, keepdims=False)

    blocks = hidden.shape[0]
    places = x_count * high_count
    kv_columns = kv_weight.shape[1]

    def whole(*shape):
        return pl.BlockSpec(shape, lambda step: (0,) * len(shape))

    attended = pl.pallas_call(
        functools.partial(attend_kernel, width, cache_len),
        grid=(blocks,),
        out_shape=jax.ShapeDtypeStruct((places, requests, head_width), bf16),
        in_specs=[
            pl.BlockSpec((1, tokens, depth), lambda step: (step, 0, 0)),
            pl.BlockSpec((depth, kv_columns), lambda step: (step, 0)),
            pl.BlockSpec((1, 1, depth), lambda step: (step, 0, 0)),
            whole(2, tokens, HEAD_DIM),
            whole(requests, head_width + kv_columns),
            whole(2, requests, HEAD_DIM),
            whole(requests, 1),
        ],
        out_specs=whole(places, requests, head_width),
        scratch_shapes=[pltpu.VMEM((tokens, kv_columns), f32), pltpu.VMEM((tokens, 1), f32)],
        compiler_params=pltpu.CompilerParams(vmem_limit_bytes=60 * 1024 * 1024),
    )(
        hidden,
        kv_weight,
        attn_gain.reshape(blocks, 1, depth),
        rope_turns(np.arange(tokens) % cache_len, np),
        picked,
        rope_turns(prompt_lengths),
        prompt_lengths[:, None],
    )

    (attended,) = phase([(2, 1), (0, 1)], attended)
    attended = lax.all_to_all(attended, ("x", "h"), 0, 0, tiled=True)
    place = jnp.stack([core, low, x, high]).astype(jnp.int32)
    smem = pl.BlockSpec(memory_space=pltpu.SMEM)
    vmem = pl.BlockSpec(memory_space=pltpu.VMEM)
    part = jax.ShapeDtypeStruct((places, half, low_count * columns), f32)
    kept, given = pl.pallas_call(
        project_kernel,
        out_shape=(part, part),
        in_specs=[smem, vmem, vmem, vmem],
        out_specs=(vmem, vmem),
        compiler_params=pltpu.CompilerParams(vmem_limit_bytes=24 * 1024 * 1024),
    )(place, attended, out_weight, out_near)
    terms = (kept + swap(given)).reshape(x_count * row_block, -1)
    updated = residual_here + rows_at(terms, y * row_block, row_block)
    for step in range(1, y_count):
        part = rows_at(terms, lax.rem(y + step, y_count) * row_block, row_block)
        updated = updated + shift(part, "y", step)
    gained = (updated * gain_here).astype(bf16)

    count = x_count * low_count * y_count
    gathered = lax.all_to_all(
        jnp.broadcast_to(gained[None], (count,) + gained.shape), ("x", "l", "y"), 0, 0, tiled=True
    )
    gathered = gathered.reshape(x_count, count // x_count * row_block, -1)

    request_order = jnp.transpose(by_place, (3, 2, 0, 1, 4))
    request_order = jnp.where(core == 0, request_order, request_order[::-1]).reshape(-1)
    weights = [vocab_blocks[d, e] for d in range(x_count) for e in range(low_count)]
    operands = [gathered, swap(gathered)] + weights
    part = jax.ShapeDtypeStruct((total_rows // high_count, vocab_cols + LANES), bf16)
    partial = pl.pallas_call(
        functools.partial(logits_kernel, (high_count, x_count, low_count, requests)),
        out_shape=(part,) * high_count,
        in_specs=[smem, vmem, vmem] + [pl.BlockSpec(memory_space=pl.ANY)] * len(operands),
        out_specs=(vmem,) * high_count,
        scratch_shapes=[pltpu.VMEM(value.shape, bf16) for value in operands]
        + [pltpu.SemaphoreType.DMA((len(operands),))],
        compiler_params=pltpu.CompilerParams(vmem_limit_bytes=60 * 1024 * 1024),
    )(place, gains, request_order[None, :], *operands)
    parts = [partial[0]] + [shift(partial[d], "h", d) for d in (2, 1, 3)]
    summed = sum(value.astype(f32) for value in parts)
    own_squares = jnp.sum(summed[:, vocab_cols : vocab_cols + 3], axis=1, keepdims=True)
    logits = summed[:, :vocab_cols] * lax.rsqrt(own_squares / width + epsilon)

    id_rows = sampled_ids.reshape(x_count, high_count, low_count, requests)
    id_rows = lax.dynamic_index_in_dim(id_rows, high, 1, keepdims=False).reshape(-1)
    first = (y * CORES + core) * vocab_local + (x * low_count + low) * vocab_cols
    column_ids = first + jnp.arange(vocab_cols, dtype=jnp.int32)
    highest = jnp.max(logits, axis=-1)
    summed_exp = jnp.sum(jnp.exp(logits - highest[:, None]), axis=-1)
    target = jnp.sum(jnp.where(column_ids[None, :] == id_rows[:, None], logits, 0.0), axis=-1)
    stats = jnp.stack([highest, summed_exp, target]).reshape(3, group, requests)
    stats = jnp.transpose(stats, (1, 0, 2)).reshape(group, 3 * requests)
    stats = jnp.pad(stats, ((0, 0), (0, LANES - 3 * requests)))
    ends = y_count * CORES
    stats = jnp.broadcast_to(stats[None], (ends, group, LANES)).reshape(ends * group, 1, LANES)
    stats = lax.all_to_all(stats, ("y", "c", "x", "l"), 0, 0, tiled=True)[:, 0]
    all_highest = stats[:, :requests]
    top = jnp.max(all_highest, axis=0)
    sum_all = jnp.sum(
        stats[:, requests : 2 * requests] * jnp.exp(all_highest - top[None, :]), axis=0
    )
    target_all = jnp.sum(stats[:, 2 * requests : 3 * requests], axis=0)
    return (target_all - top - jnp.log(sum_all))[None, :]


def solution(mesh):
    pre, wide = mesh.devices.shape
    shape = (pre // CORES, CORES, X, wide // X // LOW, LOW)
    fine = Mesh(mesh.devices.reshape(shape), ("y", "c", "x", "h", "l"))
    pre_axes = ("y", "c")
    wide_axes = ("x", "h", "l")
    return jax.shard_map(
        local,
        mesh=fine,
        in_specs=(
            P(wide_axes, pre_axes),
            P(),
            P(None, pre_axes),
            P(wide_axes),
            P(wide_axes),
            P(None, wide_axes, pre_axes),
            P(None, wide_axes, pre_axes),
            P(pre_axes, wide_axes),
            P(None, None, wide_axes),
            P(wide_axes),
            P(wide_axes, pre_axes),
            P(),
        ),
        out_specs=P(None, wide_axes),
        check_vma=False,
    )
```
